128 devices in a mesh: section: 8 (over z, x_hi), ctx: 8 (over y, core), head: 2 (over x_lo).
Axes of the slice: x: 4 (x_hi: 2, x_lo: 2; x = x_hi * 2 + x_lo), y: 4, z: 4, core: 2. Of those that a mesh axis runs over, the one named last changes fastest.
Arguments:
- queries: bfloat16 [8, 2560, 5120], P('section', 'ctx', 'head'), may hold values from -6 to 6
- out_grad: bfloat16 [8, 2560, 5120], P('section', 'ctx', 'head'), may hold values from -12 to 12
- keys: bfloat16 [2560, 1024], P(('section', 'ctx'), 'head'), may hold values from -6 to 6
- values: bfloat16 [2560, 1024], P(('section', 'ctx'), 'head'), may hold values from -6 to 6
Outputs:
- query_grad: bfloat16 [8, 2560, 5120], P('section', 'ctx', 'head')
- key_grad: bfloat16 [2560, 1024], P(('section', 'ctx'), 'head')
- value_grad: bfloat16 [2560, 1024], P(('section', 'ctx'), 'head')
The draws below stay inside these ranges and needn't reach their ends.
All inputs are finite; a program needn't handle non-finite values.
Results may differ from the reference program's by a relative error of at most 0.0089.
Values may be sent and summed in bfloat16 or wider, within the bound.
A program may use at most 64 MiB of HBM per device.

```python
import jax
import jax.numpy as jnp
from jax import lax

HEADS = 40
KV_HEADS = 8
HEAD_DIM = 128
LAYERS = 8
SEQ = 2560


def draw_keys(key, part):
    key = jax.random.fold_in(key, 11)
    shape = (SEQ, KV_HEADS * HEAD_DIM)
    base = jnp.clip(jax.random.normal(key, shape, jnp.float32), -6.0, 6.0)
    return base.astype(jnp.bfloat16)


def draw_queries(key, part):
    key = jax.random.fold_in(key, 23)
    shape = (LAYERS, SEQ, HEADS * HEAD_DIM)
    base = jnp.clip(jax.random.normal(key, shape, jnp.float32), -6.0, 6.0)
    return base.astype(jnp.bfloat16)


def level_of(stream_key, dims, shards, least, largest):
    level, own = 1.0, jax.random.fold_in(stream_key, 6)
    for dim, parts in shards:
        draws = jnp.exp(jax.random.uniform(jax.random.fold_in(own, dim), (parts,), jnp.float32, least / len(shards), largest / len(shards)))
        level = level * jnp.repeat(draws, dims[dim] // parts).reshape([-1 if axis == dim else 1 for axis in range(len(dims))])
    return level


def bell_draw(own_key, shape, spread, bound, pieces=(), kind=jnp.bfloat16):
    gain = level_of(own_key, shape, pieces, -0.22, 0.18) if pieces else 1.0
    values = jax.random.normal(own_key, shape, jnp.float32) * spread * gain
    return jnp.minimum(jnp.maximum(values, -bound), bound).astype(kind)


def setup_inputs(seed: int = 0) -> dict:
    seeds = jax.random.split(jax.random.key(seed), 5)
    queries = draw_queries(jax.random.fold_in(seeds[4], 71), 0)
    out_grad = bell_draw(seeds[1], (LAYERS, SEQ, HEADS * HEAD_DIM), 2.0, 12.0, ((0, 8), (1, 8), (2, 2)))
    keys = draw_keys(jax.random.fold_in(seeds[4], 71), 0)
    values = bell_draw(seeds[3], (SEQ, KV_HEADS * HEAD_DIM), 1.0, 6.0, ((0, 64), (1, 2)))
    return dict(queries=queries, out_grad=out_grad, keys=keys, values=values)


def group_grads(query_rows, grad_rows, key_rows, value_rows):
    scale_factor = HEAD_DIM ** -0.5
    query_full = query_rows.astype(jnp.float32)
    grad_full = grad_rows.astype(jnp.float32)
    key_full = key_rows.astype(jnp.float32)
    value_full = value_rows.astype(jnp.float32)
    scores = jnp.einsum('igd,jd->gij', query_full, key_full) * scale_factor
    position = jnp.arange(SEQ, dtype=jnp.int32)
    visible = position[None, :] <= position[:, None]
    scores = jnp.where(visible[None], scores, -jnp.inf)
    row_max = scores.max(-1, keepdims=True)
    weights = jnp.exp(scores - row_max)
    soft_probs = weights / weights.sum(-1, keepdims=True)
    out_dots = jnp.einsum('igd,jd->gij', grad_full, value_full)
    row_delta = (soft_probs * out_dots).sum(-1, keepdims=True)
    score_grad = lax.optimization_barrier((soft_probs * (out_dots - row_delta)).astype(jnp.bfloat16)).astype(jnp.float32)
    probs_low = lax.optimization_barrier(soft_probs.astype(jnp.bfloat16)).astype(jnp.float32)
    query_part = scale_factor * jnp.einsum('gij,jd->igd', score_grad, key_full)
    key_part = scale_factor * jnp.einsum('gij,igd->jd', score_grad, query_full)
    value_part = jnp.einsum('gij,igd->jd', probs_low, grad_full)
    return query_part, key_part, value_part


def reference(queries, out_grad, keys, values):
    groups = HEADS // KV_HEADS
    query_all = queries.reshape(LAYERS, SEQ, KV_HEADS, groups, HEAD_DIM)
    grad_all = out_grad.reshape(LAYERS, SEQ, KV_HEADS, groups, HEAD_DIM)
    key_all = keys.reshape(SEQ, KV_HEADS, HEAD_DIM)
    value_all = values.reshape(SEQ, KV_HEADS, HEAD_DIM)

    def layer_head(flat_index):
        layer = flat_index // KV_HEADS
        kv_head = flat_index % KV_HEADS
        query_rows = query_all[layer][:, kv_head]
        grad_rows = grad_all[layer][:, kv_head]
        return group_grads(query_rows, grad_rows, key_all[:, kv_head], value_all[:, kv_head])

    query_part, key_part, value_part = lax.map(layer_head, jnp.arange(LAYERS * KV_HEADS, dtype=jnp.int32))
    query_grad = query_part.reshape(LAYERS, KV_HEADS, SEQ, groups, HEAD_DIM).transpose(0, 2, 1, 3, 4)
    query_grad = query_grad.reshape(LAYERS, SEQ, HEADS * HEAD_DIM).astype(jnp.bfloat16)
    key_grad = key_part.reshape(LAYERS, KV_HEADS, SEQ, HEAD_DIM).sum(0).transpose(1, 0, 2)
    value_grad = value_part.reshape(LAYERS, KV_HEADS, SEQ, HEAD_DIM).sum(0).transpose(1, 0, 2)
    key_grad = key_grad.reshape(SEQ, KV_HEADS * HEAD_DIM).astype(jnp.bfloat16)
    value_grad = value_grad.reshape(SEQ, KV_HEADS * HEAD_DIM).astype(jnp.bfloat16)
    return query_grad, key_grad, value_grad
```

```python
import functools

import jax
import jax.numpy as jnp
from jax import lax
from jax.experimental import pallas as pl
from jax.experimental.pallas import tpu as pltpu
from jax.sharding import PartitionSpec as P

HD = 128
LOG2E = 1.4426950408889634
bf16, f32 = jnp.bfloat16, jnp.float32
MESH = pl.DeviceIdType.MESH
Z, X, Y, C = 4, 2, 4, 2


def dot_nt(a, b):
    return lax.dot_general(a, b, (((1,), (1,)), ((), ())), preferred_element_type=f32)


def dot_tn(a, b):
    return lax.dot_general(a, b, (((0,), (0,)), ((), ())), preferred_element_type=f32)


def in_pairs(count, step):
    @pl.loop(0, count // 2)
    def _(i):
        step(2 * i)
        step(2 * i + 1)

    @pl.loop(count // 2 * 2, count)
    def _(i):
        step(i)


STREAMS = ((0, 0, 48, "yz"), (0, 48, 32, "zy"), (1, 0, 80, "zy"), (2, 0, 80, "yz"), (3, 0, 80, "zy"))


def kernel(q_hbm, do_hbm, k_in, v_in, dq_hbm, dk_out, dv_out,
           kv, qf, dof, qs, k2, vv, s_ref, d_ref, m_ref, l_ref, c_ref, dqt, dq_st,
           dk_acc, dv_acc, own, keep_z, keep_y, cs, cr, zs, zr, ys, yr, xs, xr,
           in_sem, dq_sem, gx, gs, gc, rc, rz, ry, rx):
    rows = q_hbm.shape[0]
    share = k_in.shape[0]
    heads = k_in.shape[1] // HD
    groups = q_hbm.shape[1] // k_in.shape[1]
    flat = rows * groups
    scale = HD ** -0.5
    section, ctx, half = lax.axis_index("section"), lax.axis_index("ctx"), lax.axis_index("head")
    z, x, y, c = section // X, section % X, ctx // C, ctx % C
    place = ctx
    blocks = place + 1

    def device(z, x, y, c):
        return (z * X + x, y * C + c, half)

    y_at = [device(z, x, (y + d) % Y, c) for d in range(1, Y)]
    z_at = [device((z + d) % Z, x, y, c) for d in range(1, Z)]
    x_at = device(z, 1 - x, y, c)
    c_at = device(z, x, y, 1 - c)

    def load(h, g, which):
        source, target = ((q_hbm, qf), (do_hbm, dof))[which]
        cols = pl.ds(pl.multiple_of((h * groups + g) * HD, HD), HD)
        return pltpu.make_async_copy(
            source.at[:, cols], target.at[h, pl.ds(g * rows, rows), :], in_sem.at[which, h, g])

    for h in range(heads):
        for g in range(groups):
            load(h, g, 0).start()
            load(h, g, 1).start()

    barrier = pltpu.get_barrier_semaphore()
    partners = y_at + z_at + [x_at, c_at]
    for partner in partners:
        pl.semaphore_signal(barrier, inc=1, device_id=partner, device_id_type=MESH)
    for h in range(heads):
        cols = slice(h * HD, (h + 1) * HD)
        pair = jnp.concatenate([k_in[:, cols].astype(f32), v_in[:, cols].astype(f32)], axis=0)
        kv[h, z, x, y, c] = pair.astype(bf16)
    pl.semaphore_wait(barrier, len(partners))

    def copy(src, dst, sems, index, where):
        return pltpu.make_async_remote_copy(
            src_ref=src, dst_ref=dst, send_sem=sems.at[(0,) + index], recv_sem=sems.at[(1,) + index],
            device_id=where, device_id_type=MESH)

    near = {"y": y_at, "z": z_at}

    def gather_x():
        part = kv.at[:, z, x, y, c]
        return copy(part, part, gx, (), x_at)

    def gather_step(n, step, d):
        h, first, count, order = STREAMS[n]
        some = pl.ds(first, count)
        if step == 0:
            part = kv.at[h, z, :, y, c, some]
        elif order[0] == "y":
            part = kv.at[h, z, :, :, c, some]
        else:
            part = kv.at[h, :, :, y, c, some]
        return copy(part, part, gs, (n, step, d - 1), near[order[step]][d - 1])

    def gather_c(h):
        part = kv.at[h, :, :, :, c]
        return copy(part, part, gc, (h,), c_at)

    def streams_of(h):
        return [n for n in range(len(STREAMS)) if STREAMS[n][0] == h]

    def start_step(h, step):
        for n in streams_of(h):
            for d in range(1, 4):
                gather_step(n, step, d).start()

    def end_step(h, step):
        for n in streams_of(h):
            for d in range(1, 4):
                gather_step(n, step, d).wait_recv()

    gather_x().start()
    gather_x().wait_recv()
    for h in range(heads):
        start_step(h, 0)
    end_step(0, 0)
    start_step(0, 1)
    end_step(0, 1)
    gather_c(0).start()
    for h in range(1, heads):
        end_step(h, 0)
        start_step(h, 1)

    def sum_c(h):
        return copy(cs, cr.at[h % 2], rc, (h,), c_at)

    def sum_z(h, d):
        return copy(zs.at[d - 1], zr.at[h % 2, d - 1], rz, (h, d - 1), z_at[d - 1])

    def sum_y(h, d):
        return copy(ys.at[d - 1], yr.at[h, d - 1], ry, (h, d - 1), y_at[d - 1])

    def sum_x(h):
        return copy(xs, xr.at[h], rx, (h,), x_at)

    def sum_first(h):
        @pl.when(h >= 1)
        def _():
            sum_c(h - 1).wait_send()

        for i in range(Z * X):
            for core, put in ((1 - c, True), (c, False)):
                pair = jnp.concatenate([dk_acc[i, :, core], dv_acc[i, :, core]], axis=1)
                if put:
                    cs[i // X, i % X] = pair.astype(bf16)
                else:
                    own[i // X, i % X] = pair
        sum_c(h).start()

    def sum_second(h):
        sum_c(h).wait_recv()

        @pl.when(h >= 1)
        def _():
            for d in range(1, Z):
                sum_z(h - 1, d).wait_send()

        for d in range(1, Z):
            i = (z + d) % Z
            zs[d - 1] = (own[i] + cr[h % 2, i].astype(f32)).astype(bf16)
            sum_z(h, d).start()
        keep_z[h % 2] = own[z] + cr[h % 2, z].astype(f32)

    def sum_third(h):
        for d in range(1, Z):
            sum_z(h, d).wait_recv()
        total = keep_z[h % 2]
        for d in range(1, Z):
            total = total + zr[h % 2, d - 1].astype(f32)
        keep_z[h % 2] = total

        @pl.when(h >= 1)
        def _():
            for d in range(1, Y):
                sum_y(h - 1, d).wait_send()

        for d in range(1, Y):
            ys[d - 1] = keep_z[h % 2, :, (y + d) % Y].astype(bf16)
            sum_y(h, d).start()

    def sum_fourth(h):
        for d in range(1, Y):
            sum_y(h, d).wait_recv()
        total = keep_z[h % 2, :, y]
        for d in range(1, Y):
            total = total + yr[h, d - 1].astype(f32)
        keep_y[...] = total

        @pl.when(h >= 1)
        def _():
            sum_x(h - 1).wait_send()

        xs[...] = keep_y[1 - x].astype(bf16)
        sum_x(h).start()

    def sum_last(h):
        sum_x(h).wait_recv()
        total = keep_y[x] + xr[h].astype(f32)
        cols = pl.ds(pl.multiple_of(h * HD, HD), HD)
        dk_out[:, cols] = (total[:share] * scale).astype(bf16)
        dv_out[:, cols] = total[share:].astype(bf16)

    def write_dq(h, g):
        cols = pl.ds(pl.multiple_of((h * groups + g) * HD, HD), HD)
        return pltpu.make_async_copy(
            dq_st.at[h % 2, pl.ds(g * rows, rows), :], dq_hbm.at[:, cols], dq_sem.at[h % 2, g])

    row_id = lax.rem(lax.broadcasted_iota(jnp.int32, (1, flat), 1), rows)
    key_id = lax.broadcasted_iota(jnp.int32, (rows, flat), 0)

    def head(h, carry):
        for g in range(groups):
            load(h, g, 0).wait()
            load(h, g, 1).wait()
        gather_c(h).wait_recv()
        wide = qf[h].astype(f32) * (scale * LOG2E)
        high = wide.astype(bf16)
        qs[:, :HD] = high
        qs[:, HD:] = (wide - high.astype(f32)).astype(bf16)

        @pl.loop(0, Z * X)
        def _(i):
            at = pl.ds(pl.multiple_of(i * rows, rows), rows)
            pair = kv[h, i // X, i % X].astype(f32)
            key = pair[:, :, :share].reshape(rows, HD).astype(bf16)
            k2[at, :HD] = key
            k2[at, HD:] = key
            vv[at, :] = pair[:, :, share:].reshape(rows, HD).astype(bf16)

        @pl.when(h >= 2)
        def _():
            sum_third(h - 2)

        @pl.when(h >= 3)
        def _():
            sum_last(h - 3)

        m_ref[...] = jnp.full_like(m_ref, -1e30)
        l_ref[...] = jnp.zeros_like(l_ref)
        c_ref[...] = jnp.zeros_like(c_ref)
        dqt[...] = jnp.zeros_like(dqt)

        def front(b, masked):
            at = pl.ds(pl.multiple_of(b * rows, rows), rows)
            s = dot_nt(k2[at, :], qs[...])
            if masked:
                s = jnp.where(key_id <= row_id, s, -jnp.inf)
            d = dot_nt(vv[at, :], dof[h])
            s_ref[at, :] = s
            d_ref[at, :] = d
            s = s_ref[at, :].reshape(rows // 8, 8, flat)
            d = d_ref[at, :].reshape(rows // 8, 8, flat)
            old = m_ref[...]
            new = jnp.maximum(old, s.max(0))
            fade = jnp.exp2(old - new)
            e = jnp.exp2(s - new)
            l_ref[...] = l_ref[...] * fade + e.sum(0)
            c_ref[...] = c_ref[...] * fade + (e * d).sum(0)
            m_ref[...] = new

        in_pairs(place, lambda b: front(b, False))
        front(place, True)

        for following in range(1, heads):
            @pl.when(h == following - 1)
            def _():
                end_step(following, 1)
                gather_c(following).start()

        @pl.when(h >= 1)
        def _():
            sum_second(h - 1)

        @pl.when(h >= 2)
        def _():
            sum_fourth(h - 2)

        top8 = m_ref[...]
        top = top8.max(0, keepdims=True)
        fade = jnp.exp2(top8 - top)
        total = (l_ref[...] * fade).sum(0, keepdims=True)
        lse = jnp.broadcast_to(top + jnp.log2(total), (8, flat))
        delta = jnp.broadcast_to((c_ref[...] * fade).sum(0, keepdims=True) / total, (8, flat))

        def back(b):
            at = pl.ds(pl.multiple_of(b * rows, rows), rows)
            p = jnp.exp2(s_ref[at, :].reshape(rows // 8, 8, flat) - lse)
            ds = p * (d_ref[at, :].reshape(rows // 8, 8, flat) - delta)
            p = p.reshape(rows, flat).astype(bf16)
            ds = ds.reshape(rows, flat).astype(bf16)
            dv_acc[b] = jnp.dot(p, dof[h], preferred_element_type=f32).reshape(Y, C, share, HD)
            dk_acc[b] = jnp.dot(ds, qf[h], preferred_element_type=f32).reshape(Y, C, share, HD)
            dqt[...] += dot_tn(k2[at, :HD], ds)

        in_pairs(blocks, back)

        @pl.loop(blocks, Z * X)
        def _(b):
            dv_acc[b] = jnp.zeros((Y, C, share, HD), f32)
            dk_acc[b] = jnp.zeros((Y, C, share, HD), f32)

        @pl.when(h >= 2)
        def _():
            for g in range(groups):
                write_dq(h - 2, g).wait()

        dq_st[h % 2] = (dqt[...] * scale).T.astype(bf16)
        for g in range(groups):
            write_dq(h, g).start()
        sum_first(h)
        return carry

    lax.fori_loop(0, heads, head, 0)

    last = heads - 1
    sum_third(last - 1)
    sum_second(last)
    sum_last(last - 2)
    sum_fourth(last - 1)
    sum_third(last)
    sum_last(last - 1)
    sum_fourth(last)
    sum_last(last)
    gather_x().wait_send()
    for h in range(heads):
        gather_c(h).wait_send()
        for n in streams_of(h):
            for d in range(1, 4):
                gather_step(n, 0, d).wait_send()
                gather_step(n, 1, d).wait_send()
    sum_c(last).wait_send()
    sum_x(last).wait_send()
    for d in range(1, 4):
        sum_z(last, d).wait_send()
        sum_y(last, d).wait_send()
    for h in (last - 1, last):
        for g in range(groups):
            write_dq(h, g).wait()


def shards(queries, out_grad, keys, values):
    _, rows, cols = queries.shape
    share, key_cols = keys.shape
    heads = key_cols // HD
    groups = cols // key_cols
    flat = rows * groups
    seq = rows * Z * X
    pair = (2 * share, HD)
    V = pltpu.VMEM
    sem = pltpu.SemaphoreType.DMA
    any_space = pl.BlockSpec(memory_space=pl.ANY)
    in_vmem = pl.BlockSpec(memory_space=pltpu.VMEM)
    dq, dk, dv = pl.pallas_call(
        kernel,
        in_specs=[any_space, any_space, in_vmem, in_vmem],
        out_specs=[any_space, in_vmem, in_vmem],
        out_shape=[jax.ShapeDtypeStruct((rows, cols), bf16),
                   jax.ShapeDtypeStruct((share, key_cols), bf16),
                   jax.ShapeDtypeStruct((share, key_cols), bf16)],
        scratch_shapes=[
            V((heads, Z, X, Y, C) + pair, bf16),
            V((heads, flat, HD), bf16), V((heads, flat, HD), bf16),
            V((flat, 2 * HD), bf16), V((seq, 2 * HD), bf16), V((seq, HD), bf16),
            V((seq, flat), f32), V((seq, flat), f32),
            V((8, flat), f32), V((8, flat), f32), V((8, flat), f32),
            V((HD, flat), f32), V((2, flat, HD), bf16),
            V((Z * X, Y, C, share, HD), f32), V((Z * X, Y, C, share, HD), f32),
            V((Z, X, Y) + pair, f32), V((2, X, Y) + pair, f32), V((X,) + pair, f32),
            V((Z, X, Y) + pair, bf16), V((2, Z, X, Y) + pair, bf16),
            V((Z - 1, X, Y) + pair, bf16), V((2, Z - 1, X, Y) + pair, bf16),
            V((Y - 1, X) + pair, bf16), V((heads, Y - 1, X) + pair, bf16),
            V(pair, bf16), V((heads,) + pair, bf16),
            sem((2, heads, groups)), sem((2, groups)),
            sem((2,)), sem((2, len(STREAMS), 2, 3)), sem((2, heads)),
            sem((2, heads)), sem((2, heads, Z - 1)), sem((2, heads, Y - 1)), sem((2, heads)),
        ],
        compiler_params=pltpu.CompilerParams(
            collective_id=0, has_side_effects=True, vmem_limit_bytes=65400 << 10),
    )(queries[0], out_grad[0], keys, values)
    return dq[None], dk, dv


def solution(mesh):
    wide = P("section", "ctx", "head")
    tall = P(("section", "ctx"), "head")
    return jax.shard_map(shards, mesh=mesh, in_specs=(wide, wide, tall, tall),
                         out_specs=(wide, tall, tall), check_vma=False)
```

```python
import functools

import jax
import jax.numpy as jnp
from jax import lax
from jax.experimental import pallas as pl
from jax.experimental.pallas import tpu as pltpu
from jax.sharding import PartitionSpec as P

HD = 128
LOG2E = 1.4426950408889634
bf16, f32 = jnp.bfloat16, jnp.float32
MESH = pl.DeviceIdType.MESH
Z, X, Y, C = 4, 2, 4, 2


def dot_nt(a, b):
    return lax.dot_general(a, b, (((1,), (1,)), ((), ())), preferred_element_type=f32)


def dot_tn(a, b):
    return lax.dot_general(a, b, (((0,), (0,)), ((), ())), preferred_element_type=f32)


def in_pairs(count, step):
    @pl.loop(0, count // 2)
    def _(i):
        step(2 * i)
        step(2 * i + 1)

    @pl.loop(count // 2 * 2, count)
    def _(i):
        step(i)


CTX = Y * C
SHIP = ((0, 4, 0), (5, 5, 1), (6, 7, 2))


def kernel(q_hbm, do_hbm, k_in, v_in, dq_hbm, dk_out, dv_out,
           kv, qf, dof, fq, fdo, qs, k2, vv, s_ref, d_ref, m_ref, l_ref, c_ref, dqt, dq_st, fdq_st,
           dk_acc, dv_acc, own_sum, keep_b, keep_y, cs, cr, bs, br, ys, yr,
           in_sem, dq_sem, ship_sem, back_sem, gy, gb, gc, rc, rb, ry):
    rows = q_hbm.shape[0]
    share = k_in.shape[0]
    heads = k_in.shape[1] // HD
    groups = q_hbm.shape[1] // k_in.shape[1]
    flat = rows * groups
    scale = HD ** -0.5
    section, ctx, half = lax.axis_index("section"), lax.axis_index("ctx"), lax.axis_index("head")
    z, x, y, c = section // X, section % X, ctx // C, ctx % C

    def device(z, x, y, c):
        return (z * X + x, y * C + c, half)

    y_at = [device(z, x, (y + d) % Y, c) for d in range(1, Y)]
    c_at = device(z, x, y, 1 - c)
    others = [(dz, dx) for dz in range(Z) for dx in range(X) if dz or dx]
    block_of = [((z + dz) % Z, (x + dx) % X) for dz, dx in others]
    block_at = [device(bz, bx, y, c) for bz, bx in block_of]

    def load(h, g, which):
        source, target = ((q_hbm, qf), (do_hbm, dof))[which]
        cols = pl.ds(pl.multiple_of((h * groups + g) * HD, HD), HD)
        return pltpu.make_async_copy(
            source.at[:, cols], target.at[h, pl.ds(g * rows, rows), :], in_sem.at[which, h, g])

    mirror = (section, CTX - 1 - ctx, half)

    def shipped(h, i, count, which):
        source, target = ((q_hbm, fq), (do_hbm, fdo))[which]
        cols = pl.ds(pl.multiple_of(((h + 1) * groups - count + i) * HD, HD), HD)
        return pltpu.make_async_remote_copy(
            src_ref=source.at[:, cols], dst_ref=target.at[h, pl.ds(i * rows, rows), :],
            send_sem=ship_sem.at[0, which, h, i], recv_sem=ship_sem.at[1, which, h, i],
            device_id=mirror, device_id_type=MESH)

    def returned(h, i, count):
        cols = pl.ds(pl.multiple_of(((h + 1) * groups - count + i) * HD, HD), HD)
        return pltpu.make_async_remote_copy(
            src_ref=fdq_st.at[h % 2, pl.ds(i * rows, rows), :], dst_ref=dq_hbm.at[:, cols],
            send_sem=back_sem.at[0, h, i], recv_sem=back_sem.at[1, h, i],
            device_id=mirror, device_id_type=MESH)

    owners = [(low <= ctx, ctx <= high, count) for low, high, count in SHIP]
    owners = [(jnp.logical_and(over, under), count) for over, under, count in owners]
    helpers = [(low <= CTX - 1 - ctx, CTX - 1 - ctx <= high, count) for low, high, count in SHIP]
    helpers = [(jnp.logical_and(over, under), count) for over, under, count in helpers if count]

    for is_owner, count in owners:
        @pl.when(is_owner)
        def _():
            for h in range(heads):
                for g in range(groups - count):
                    load(h, g, 0).start()
                    load(h, g, 1).start()

    barrier = pltpu.get_barrier_semaphore()
    partners = y_at + block_at + [c_at, mirror]
    for partner in partners:
        pl.semaphore_signal(barrier, inc=1, device_id=partner, device_id_type=MESH)
    for h in range(heads):
        cols = slice(h * HD, (h + 1) * HD)
        pair = jnp.concatenate([k_in[:, cols].astype(f32), v_in[:, cols].astype(f32)], axis=0)
        kv[h, z, x, y, c] = pair.astype(bf16)
    pl.semaphore_wait(barrier, len(partners))

    def copy(src, dst, sems, index, where):
        return pltpu.make_async_remote_copy(
            src_ref=src, dst_ref=dst, send_sem=sems.at[(0,) + index], recv_sem=sems.at[(1,) + index],
            device_id=where, device_id_type=MESH)

    def gather_y(d):
        part = kv.at[:, z, x, y, c]
        return copy(part, part, gy, (d - 1,), y_at[d - 1])

    def gather_b(h, i):
        part = kv.at[h, z, x, :, c]
        return copy(part, part, gb, (h, i), block_at[i])

    def gather_c(h):
        part = kv.at[h, :, :, :, c]
        return copy(part, part, gc, (h,), c_at)

    def start_blocks(h):
        for i in range(len(others)):
            gather_b(h, i).start()

    def end_blocks(h):
        for i in range(len(others)):
            gather_b(h, i).wait_recv()

    def ship(heads_now):
        for is_owner, count in owners:
            if count:
                @pl.when(is_owner)
                def _():
                    for h in heads_now:
                        for i in range(count):
                            shipped(h, i, count, 0).start()
                            shipped(h, i, count, 1).start()

    for d in range(1, Y):
        gather_y(d).start()
    ship([0])
    for d in range(1, Y):
        gather_y(d).wait_recv()
    start_blocks(0)
    ship(range(1, heads))
    end_blocks(0)
    gather_c(0).start()
    start_blocks(1)
    start_blocks(2)

    def sum_c(h):
        return copy(cs, cr.at[h % 2], rc, (h,), c_at)

    def sum_b(h, i):
        return copy(bs.at[i], br.at[h, i], rb, (h, i), block_at[i])

    def sum_y(h, d):
        return copy(ys.at[d - 1], yr.at[h, d - 1], ry, (h, d - 1), y_at[d - 1])

    def sum_first(h):
        @pl.when(h >= 1)
        def _():
            sum_c(h - 1).wait_send()

        for i in range(Z * X):
            for core, put in ((1 - c, True), (c, False)):
                pair = jnp.concatenate([dk_acc[i, :, core], dv_acc[i, :, core]], axis=1)
                if put:
                    cs[i // X, i % X] = pair.astype(bf16)
                else:
                    own_sum[i // X, i % X] = pair
        sum_c(h).start()

    def sum_second(h):
        sum_c(h).wait_recv()

        @pl.when(h >= 1)
        def _():
            for i in range(len(others)):
                sum_b(h - 1, i).wait_send()

        for i, (bz, bx) in enumerate(block_of):
            bs[i] = (own_sum[bz, bx] + cr[h % 2, bz, bx].astype(f32)).astype(bf16)
            sum_b(h, i).start()
        keep_b[h % 2] = own_sum[z, x] + cr[h % 2, z, x].astype(f32)

    def sum_third(h):
        total = keep_b[h % 2]
        for i in range(len(others)):
            sum_b(h, i).wait_recv()
            total = total + br[h, i].astype(f32)

        @pl.when(h >= 1)
        def _():
            for d in range(1, Y):
                sum_y(h - 1, d).wait_send()

        keep_y[...] = total
        for d in range(1, Y):
            ys[d - 1] = keep_y[(y + d) % Y].astype(bf16)
            sum_y(h, d).start()

    def sum_last(h):
        total = keep_y[y]
        for d in range(1, Y):
            sum_y(h, d).wait_recv()
            total = total + yr[h, d - 1].astype(f32)
        cols = pl.ds(pl.multiple_of(h * HD, HD), HD)
        dk_out[:, cols] = (total[:share] * scale).astype(bf16)
        dv_out[:, cols] = total[share:].astype(bf16)

    def write_dq(h, g):
        cols = pl.ds(pl.multiple_of((h * groups + g) * HD, HD), HD)
        return pltpu.make_async_copy(
            dq_st.at[h % 2, pl.ds(g * rows, rows), :], dq_hbm.at[:, cols], dq_sem.at[h % 2, g])

    def lanes_of(width):
        return [(j, min(HD, width - j)) for j in range(0, width, HD)]

    def begin(width, place, q_part, do_part):
        lanes = lanes_of(width)
        wide = q_part[...].astype(f32) * (scale * LOG2E)
        high = wide.astype(bf16)
        qs[:width, :HD] = high
        qs[:width, HD:] = (wide - high.astype(f32)).astype(bf16)
        m_ref[:, :width] = jnp.full((8, width), -1e30, f32)
        l_ref[:, :width] = jnp.zeros((8, width), f32)
        c_ref[:, :width] = jnp.zeros((8, width), f32)
        dqt[:, :width] = jnp.zeros((HD, width), f32)

        def front(b, masked):
            at = pl.ds(pl.multiple_of(b * rows, rows), rows)
            s = dot_nt(k2[at, :], qs[:width, :])
            if masked:
                row_id = lax.rem(lax.broadcasted_iota(jnp.int32, (1, width), 1), rows)
                key_id = lax.broadcasted_iota(jnp.int32, (rows, width), 0)
                s = jnp.where(key_id <= row_id, s, -jnp.inf)
            d = dot_nt(vv[at, :], do_part[...])
            for n, (j, w) in enumerate(lanes):
                s_ref[b * len(lanes) + n, :, :w] = s[:, j:j + w]
                d_ref[b * len(lanes) + n, :, :w] = d[:, j:j + w]
            for n, (j, w) in enumerate(lanes):
                s = s_ref[b * len(lanes) + n, :, :w].reshape(rows // 8, 8, w)
                d = d_ref[b * len(lanes) + n, :, :w].reshape(rows // 8, 8, w)
                some = slice(j, j + w)
                old = m_ref[:, some]
                new = jnp.maximum(old, s.max(0))
                fade = jnp.exp2(old - new)
                e = jnp.exp2(s - new)
                l_ref[:, some] = l_ref[:, some] * fade + e.sum(0)
                c_ref[:, some] = c_ref[:, some] * fade + (e * d).sum(0)
                m_ref[:, some] = new

        in_pairs(place, lambda b: front(b, False))
        front(place, True)
        top8 = m_ref[:, :width]
        top = top8.max(0, keepdims=True)
        fade = jnp.exp2(top8 - top)
        total = (l_ref[:, :width] * fade).sum(0, keepdims=True)
        m_ref[:, :width] = jnp.broadcast_to(top + jnp.log2(total), (8, width))
        l_ref[:, :width] = jnp.broadcast_to(
            (c_ref[:, :width] * fade).sum(0, keepdims=True) / total, (8, width))

    def finish(width, place, q_part, do_part, own_part):
        lanes = lanes_of(width)

        def back(b):
            at = pl.ds(pl.multiple_of(b * rows, rows), rows)
            ps, dss = [], []
            for n, (j, w) in enumerate(lanes):
                s = s_ref[b * len(lanes) + n, :, :w].reshape(rows // 8, 8, w)
                d = d_ref[b * len(lanes) + n, :, :w].reshape(rows // 8, 8, w)
                p = jnp.exp2(s - m_ref[:, j:j + w])
                ds = p * (d - l_ref[:, j:j + w])
                ps.append(p.reshape(rows, w).astype(bf16))
                dss.append(ds.reshape(rows, w).astype(bf16))
            p, ds = jnp.concatenate(ps, axis=1), jnp.concatenate(dss, axis=1)
            dv = jnp.dot(p, do_part[...], preferred_element_type=f32).reshape(Y, C, share, HD)
            dk = jnp.dot(ds, q_part[...], preferred_element_type=f32).reshape(Y, C, share, HD)
            if own_part:
                dv_acc[b] = dv
                dk_acc[b] = dk
            else:
                dv_acc[b] += dv
                dk_acc[b] += dk
            dqt[:, :width] += dot_tn(k2[at, :HD], ds)

        in_pairs(place + 1, back)

    def head(h, carry):
        gather_c(h).wait_recv()

        @pl.loop(0, Z * X)
        def _(i):
            at = pl.ds(pl.multiple_of(i * rows, rows), rows)
            pair = kv[h, i // X, i % X].astype(f32)
            key = pair[:, :, :share].reshape(rows, HD).astype(bf16)
            k2[at, :HD] = key
            k2[at, HD:] = key
            vv[at, :] = pair[:, :, share:].reshape(rows, HD).astype(bf16)

        @pl.when(h >= 3)
        def _():
            sum_last(h - 3)

        def own(count):
            width = (groups - count) * rows
            return width, ctx, qf.at[h, :width], dof.at[h, :width]

        def foreign(count):
            width = count * rows
            return width, CTX - 1 - ctx, fq.at[h, :width], fdo.at[h, :width]

        def own_end(count):
            width = (groups - count) * rows
            finish(*own(count), True)

            @pl.when(h >= 2)
            def _():
                for g in range(groups - count):
                    write_dq(h - 2, g).wait()

            dq_st[h % 2, :width] = (dqt[:, :width] * scale).T.astype(bf16)
            for g in range(groups - count):
                write_dq(h, g).start()

            @pl.loop(ctx + 1, Z * X)
            def _(b):
                dv_acc[b] = jnp.zeros((Y, C, share, HD), f32)
                dk_acc[b] = jnp.zeros((Y, C, share, HD), f32)

        def foreign_begin(count):
            for i in range(count):
                shipped(h, i, count, 0).wait_recv()
                shipped(h, i, count, 1).wait_recv()
            begin(*foreign(count))

        def foreign_end(count):
            width = count * rows
            finish(*foreign(count), False)

            @pl.when(h >= 2)
            def _():
                for i in range(count):
                    returned(h - 2, i, count).wait_send()

            fdq_st[h % 2, :width] = (dqt[:, :width] * scale).T.astype(bf16)
            for i in range(count):
                returned(h, i, count).start()

        for is_owner, count in owners:
            @pl.when(is_owner)
            def _():
                for g in range(groups - count):
                    load(h, g, 0).wait()
                    load(h, g, 1).wait()
                begin(*own(count))

        @pl.when(ctx <= 1)
        def _():
            own_end(0)
            foreign_begin(2)

        for following in range(1, heads):
            @pl.when(h == following - 1)
            def _():
                end_blocks(following)
                gather_c(following).start()
                if following == 1:
                    start_blocks(3)

        @pl.when(h >= 1)
        def _():
            sum_second(h - 1)

        @pl.when(h >= 2)
        def _():
            sum_third(h - 2)

        for is_owner, count in owners:
            @pl.when(jnp.logical_and(is_owner, ctx >= 2))
            def _():
                own_end(count)

        @pl.when(ctx <= 1)
        def _():
            foreign_end(2)

        @pl.when(ctx == 2)
        def _():
            foreign_begin(1)
            foreign_end(1)

        sum_first(h)
        return carry

    lax.fori_loop(0, heads, head, 0)

    last = heads - 1
    sum_second(last)
    sum_last(last - 2)
    sum_third(last - 1)
    sum_last(last - 1)
    sum_third(last)
    sum_last(last)
    for d in range(1, Y):
        gather_y(d).wait_send()
        sum_y(last, d).wait_send()
    for h in range(heads):
        gather_c(h).wait_send()
        for i in range(len(others)):
            gather_b(h, i).wait_send()
    sum_c(last).wait_send()
    for i in range(len(others)):
        sum_b(last, i).wait_send()
    for is_owner, count in owners:
        @pl.when(is_owner)
        def _():
            for h in range(heads):
                for i in range(count):
                    shipped(h, i, count, 0).wait_send()
                    shipped(h, i, count, 1).wait_send()
                    returned(h, i, count).wait_recv()
            for h in (last - 1, last):
                for g in range(groups - count):
                    write_dq(h, g).wait()
    for is_helper, count in helpers:
        @pl.when(is_helper)
        def _():
            for h in (last - 1, last):
                for i in range(count):
                    returned(h, i, count).wait_send()


def shards(queries, out_grad, keys, values):
    _, rows, cols = queries.shape
    share, key_cols = keys.shape
    heads = key_cols // HD
    groups = cols // key_cols
    flat = rows * groups
    seq = rows * Z * X
    pair = (2 * share, HD)
    V = pltpu.VMEM
    sem = pltpu.SemaphoreType.DMA
    any_space = pl.BlockSpec(memory_space=pl.ANY)
    in_vmem = pl.BlockSpec(memory_space=pltpu.VMEM)
    dq, dk, dv = pl.pallas_call(
        kernel,
        in_specs=[any_space, any_space, in_vmem, in_vmem],
        out_specs=[any_space, in_vmem, in_vmem],
        out_shape=[jax.ShapeDtypeStruct((rows, cols), bf16),
                   jax.ShapeDtypeStruct((share, key_cols), bf16),
                   jax.ShapeDtypeStruct((share, key_cols), bf16)],
        scratch_shapes=[
            V((heads, Z, X, Y, C) + pair, bf16),
            V((heads, flat, HD), bf16), V((heads, flat, HD), bf16),
            V((heads, 2 * rows, HD), bf16), V((heads, 2 * rows, HD), bf16),
            V((flat, 2 * HD), bf16), V((seq, 2 * HD), bf16), V((seq, HD), bf16),
            V((65, rows, HD), f32), V((65, rows, HD), f32),
            V((8, flat), f32), V((8, flat), f32), V((8, flat), f32),
            V((HD, flat), f32), V((2, flat, HD), bf16), V((2, 2 * rows, HD), bf16),
            V((Z * X, Y, C, share, HD), f32), V((Z * X, Y, C, share, HD), f32),
            V((Z, X, Y) + pair, f32), V((2, Y) + pair, f32), V((Y,) + pair, f32),
            V((Z, X, Y) + pair, bf16), V((2, Z, X, Y) + pair, bf16),
            V((Z * X - 1, Y) + pair, bf16), V((heads, Z * X - 1, Y) + pair, bf16),
            V((Y - 1,) + pair, bf16), V((heads, Y - 1) + pair, bf16),
            sem((2, heads, groups)), sem((2, groups)), sem((2, 2, heads, 2)), sem((2, heads, 2)),
            sem((2, Y - 1)), sem((2, heads, Z * X - 1)), sem((2, heads)),
            sem((2, heads)), sem((2, heads, Z * X - 1)), sem((2, heads, Y - 1)),
        ],
        compiler_params=pltpu.CompilerParams(
            collective_id=0, has_side_effects=True, vmem_limit_bytes=65400 << 10),
    )(queries[0], out_grad[0], keys, values)
    return dq[None], dk, dv


def solution(mesh):
    wide = P("section", "ctx", "head")
    tall = P(("section", "ctx"), "head")
    return jax.shard_map(shards, mesh=mesh, in_specs=(wide, wide, tall, tall),
                         out_specs=(wide, tall, tall), check_vma=False)
```

```python
import functools

import jax
import jax.numpy as jnp
from jax import lax
from jax.experimental import pallas as pl
from jax.experimental.pallas import tpu as pltpu
from jax.sharding import PartitionSpec as P

HD = 128
LOG2E = 1.4426950408889634
bf16, f32 = jnp.bfloat16, jnp.float32
MESH = pl.DeviceIdType.MESH
Z, X, Y, C = 4, 2, 4, 2


def dot_nt(a, b):
    return lax.dot_general(a, b, (((1,), (1,)), ((), ())), preferred_element_type=f32)


def dot_tn(a, b):
    return lax.dot_general(a, b, (((0,), (0,)), ((), ())), preferred_element_type=f32)


def in_groups(count, step, sizes):
    done = 0
    for size in sizes:
        @pl.loop(done // size, count // size)
        def _(i):
            for n in range(size):
                step(size * i + n)

        done = count // size * size


CTX = Y * C
ALONG_Y_LAST = (1, 3)
CUT = 48
SHIP = ((0, 4, 0), (5, 5, 1), (6, 7, 2))


def kernel(q_hbm, do_hbm, k_in, v_in, dq_hbm, dk_out, dv_out,
           kv, qf, dof, fq, fdo, qs, k2, vv, s_ref, d_ref, m_ref, l_ref, c_ref, dqt, dq_st, fdq_st,
           dk_acc, dv_acc, own_sum, keep_b, keep_y, cs, cr, bs, br, ys, yr, keep_t, ty, tyr, tb, tbr,
           in_sem, dq_sem, ship_sem, back_sem, gy, gb, gc, rc, rb, ry, ra, rc2):
    rows = q_hbm.shape[0]
    share = k_in.shape[0]
    heads = k_in.shape[1] // HD
    groups = q_hbm.shape[1] // k_in.shape[1]
    flat = rows * groups
    last = heads - 1
    scale = HD ** -0.5
    section, ctx, half = lax.axis_index("section"), lax.axis_index("ctx"), lax.axis_index("head")
    z, x, y, c = section // X, section % X, ctx // C, ctx % C

    def device(z, x, y, c):
        return (z * X + x, y * C + c, half)

    y_at = [device(z, x, (y + d) % Y, c) for d in range(1, Y)]
    c_at = device(z, x, y, 1 - c)
    others = [(dz, dx) for dz in range(Z) for dx in range(X) if dz or dx]
    block_of = [((z + dz) % Z, (x + dx) % X) for dz, dx in others]
    block_at = [device(bz, bx, y, c) for bz, bx in block_of]

    def load(h, g, which):
        source, target = ((q_hbm, qf), (do_hbm, dof))[which]
        cols = pl.ds(pl.multiple_of((h * groups + g) * HD, HD), HD)
        return pltpu.make_async_copy(
            source.at[:, cols], target.at[h, pl.ds(g * rows, rows), :], in_sem.at[which, h, g])

    mirror = (section, CTX - 1 - ctx, half)

    def shipped(h, i, count, which):
        source, target = ((q_hbm, fq), (do_hbm, fdo))[which]
        cols = pl.ds(pl.multiple_of(((h + 1) * groups - count + i) * HD, HD), HD)
        return pltpu.make_async_remote_copy(
            src_ref=source.at[:, cols], dst_ref=target.at[h, pl.ds(i * rows, rows), :],
            send_sem=ship_sem.at[0, which, h, i], recv_sem=ship_sem.at[1, which, h, i],
            device_id=mirror, device_id_type=MESH)

    def returned(h, i, count):
        cols = pl.ds(pl.multiple_of(((h + 1) * groups - count + i) * HD, HD), HD)
        return pltpu.make_async_remote_copy(
            src_ref=fdq_st.at[h % 2, pl.ds(i * rows, rows), :], dst_ref=dq_hbm.at[:, cols],
            send_sem=back_sem.at[0, h, i], recv_sem=back_sem.at[1, h, i],
            device_id=mirror, device_id_type=MESH)

    owners = [(low <= ctx, ctx <= high, count) for low, high, count in SHIP]
    owners = [(jnp.logical_and(over, under), count) for over, under, count in owners]
    helpers = [(low <= CTX - 1 - ctx, CTX - 1 - ctx <= high, count) for low, high, count in SHIP]
    helpers = [(jnp.logical_and(over, under), count) for over, under, count in helpers if count]

    for is_owner, count in owners:
        @pl.when(is_owner)
        def _():
            for h in range(heads):
                for g in range(groups - count):
                    load(h, g, 0).start()
                    load(h, g, 1).start()

    barrier = pltpu.get_barrier_semaphore()
    partners = y_at + block_at + [c_at, mirror]
    for partner in partners:
        pl.semaphore_signal(barrier, inc=1, device_id=partner, device_id_type=MESH)
    for h in range(heads):
        cols = slice(h * HD, (h + 1) * HD)
        pair = jnp.concatenate([k_in[:, cols].astype(f32), v_in[:, cols].astype(f32)], axis=0)
        kv[h, z, x, y, c] = pair.astype(bf16)
    pl.semaphore_wait(barrier, len(partners))

    def copy(src, dst, sems, index, where):
        return pltpu.make_async_remote_copy(
            src_ref=src, dst_ref=dst, send_sem=sems.at[(0,) + index], recv_sem=sems.at[(1,) + index],
            device_id=where, device_id_type=MESH)

    def gather_y(h, d):
        part = kv.at[h, :, :, y, c] if h in ALONG_Y_LAST else kv.at[h, z, x, y, c]
        return copy(part, part, gy, (h, d - 1), y_at[d - 1])

    def gather_b(h, i):
        part = kv.at[h, z, x, y, c] if h in ALONG_Y_LAST else kv.at[h, z, x, :, c]
        return copy(part, part, gb, (h, i), block_at[i])

    def gather_c(h):
        part = kv.at[h, :, :, :, c]
        return copy(part, part, gc, (h,), c_at)

    def moves(h, step):
        if (h in ALONG_Y_LAST) == (step == 0):
            return [gather_b(h, i) for i in range(len(others))]
        return [gather_y(h, d) for d in range(1, Y)]

    def start(h, step):
        for move in moves(h, step):
            move.start()

    def end(h, step):
        for move in moves(h, step):
            move.wait_recv()

    def ship(heads_now):
        for is_owner, count in owners:
            if count:
                @pl.when(is_owner)
                def _():
                    for h in heads_now:
                        for i in range(count):
                            shipped(h, i, count, 0).start()
                            shipped(h, i, count, 1).start()

    start(0, 0)
    start(1, 0)
    ship([0])
    end(0, 0)
    start(0, 1)
    end(1, 0)
    start(1, 1)
    start(2, 0)
    start(3, 0)
    ship([1])
    end(0, 1)
    gather_c(0).start()
    end(2, 0)
    start(2, 1)
    ship(range(2, heads))

    def sum_c(h):
        return copy(cs, cr.at[h % 2], rc, (h,), c_at)

    def sum_b(h, i):
        return copy(bs.at[i], br.at[h, i], rb, (h, i), block_at[i])

    def sum_y(h, d):
        return copy(ys.at[d - 1], yr.at[h, d - 1], ry, (h, d - 1), y_at[d - 1])

    def sum_first(h):
        @pl.when(h >= 1)
        def _():
            sum_c(h - 1).wait_send()

        for i in range(Z * X):
            for core, put in ((1 - c, True), (c, False)):
                pair = jnp.concatenate([dk_acc[i, :, core], dv_acc[i, :, core]], axis=1)
                if put:
                    cs[i // X, i % X] = pair.astype(bf16)
                else:
                    own_sum[i // X, i % X] = pair
        sum_c(h).start()

    def sum_second(h):
        sum_c(h).wait_recv()

        @pl.when(h >= 1)
        def _():
            for i in range(len(others)):
                sum_b(h - 1, i).wait_send()

        for i, (bz, bx) in enumerate(block_of):
            bs[i] = (own_sum[bz, bx] + cr[h % 2, bz, bx].astype(f32)).astype(bf16)
            sum_b(h, i).start()
        keep_b[h % 2] = own_sum[z, x] + cr[h % 2, z, x].astype(f32)

    def sum_third(h):
        total = keep_b[h % 2]
        for i in range(len(others)):
            sum_b(h, i).wait_recv()
            total = total + br[h, i].astype(f32)

        @pl.when(h >= 1)
        def _():
            for d in range(1, Y):
                sum_y(h - 1, d).wait_send()

        keep_y[...] = total
        for d in range(1, Y):
            ys[d - 1] = keep_y[(y + d) % Y].astype(bf16)
            sum_y(h, d).start()

    def sum_last(h):
        total = keep_y[y]
        for d in range(1, Y):
            sum_y(h, d).wait_recv()
            total = total + yr[h, d - 1].astype(f32)
        write_out(h, total)

    def write_out(h, total):
        cols = pl.ds(pl.multiple_of(h * HD, HD), HD)
        dk_out[:, cols] = (total[:share] * scale).astype(bf16)
        dv_out[:, cols] = total[share:].astype(bf16)

    def head_rows(ref):
        return ref.at[:, pl.ds(0, CUT), :]

    def tail_b(i):
        return copy(head_rows(bs.at[i]), head_rows(br.at[last, i]), rb, (last, i), block_at[i])

    def tail_y(d):
        return copy(ys.at[d - 1, pl.ds(0, CUT), :], yr.at[last, d - 1, pl.ds(0, CUT), :], ry,
                    (last, d - 1), y_at[d - 1])

    def tail_y_first(d):
        return copy(ty.at[d - 1], tyr.at[d - 1], ra, (d - 1,), y_at[d - 1])

    def tail_b_last(i):
        return copy(tb.at[i], tbr.at[i], rc2, (i,), block_at[i])

    def tail_first():
        for i in range(len(others)):
            sum_b(last - 1, i).wait_send()
        sum_c(last).wait_recv()
        slot = last % 2
        for d in range(1, Y):
            at = (y + d) % Y
            ty[d - 1] = (own_sum[:, :, at, CUT:] + cr[slot, :, :, at, CUT:].astype(f32)).astype(bf16)
            tail_y_first(d).start()
        for i, (bz, bx) in enumerate(block_of):
            bs[i, :, :CUT] = (own_sum[bz, bx, :, :CUT] + cr[slot, bz, bx, :, :CUT].astype(f32)).astype(bf16)
            tail_b(i).start()
        keep_b[slot, :, :CUT] = own_sum[z, x, :, :CUT] + cr[slot, z, x, :, :CUT].astype(f32)
        keep_t[...] = own_sum[:, :, y, CUT:] + cr[slot, :, :, y, CUT:].astype(f32)

    def tail_second():
        total = keep_t[...]
        for d in range(1, Y):
            tail_y_first(d).wait_recv()
            total = total + tyr[d - 1].astype(f32)
        keep_t[...] = total
        for i, (bz, bx) in enumerate(block_of):
            tb[i] = keep_t[bz, bx].astype(bf16)
            tail_b_last(i).start()
        total = keep_b[last % 2, :, :CUT]
        for i in range(len(others)):
            tail_b(i).wait_recv()
            total = total + br[last, i, :, :CUT].astype(f32)
        keep_y[:, :CUT] = total
        for d in range(1, Y):
            sum_y(last - 1, d).wait_send()
            ys[d - 1, :CUT] = keep_y[(y + d) % Y, :CUT].astype(bf16)
            tail_y(d).start()

    def tail_third():
        below = keep_t[z, x]
        for i in range(len(others)):
            tail_b_last(i).wait_recv()
            below = below + tbr[i].astype(f32)
        above = keep_y[y, :CUT]
        for d in range(1, Y):
            tail_y(d).wait_recv()
            above = above + yr[last, d - 1, :CUT].astype(f32)
        write_out(last, jnp.concatenate([above, below], axis=0))

    def write_dq(h, g):
        cols = pl.ds(pl.multiple_of((h * groups + g) * HD, HD), HD)
        return pltpu.make_async_copy(
            dq_st.at[h % 2, pl.ds(g * rows, rows), :], dq_hbm.at[:, cols], dq_sem.at[h % 2, g])

    def lanes_of(width):
        return [(j, min(HD, width - j)) for j in range(0, width, HD)]

    def sizes_of(width):
        return (4, 2, 1) if width <= 3 * rows else (2, 1)

    def begin(width, place, q_part, do_part):
        lanes = lanes_of(width)
        wide = q_part[...].astype(f32) * (scale * LOG2E)
        high = wide.astype(bf16)
        qs[:width, :HD] = high
        qs[:width, HD:] = (wide - high.astype(f32)).astype(bf16)
        m_ref[:, :width] = jnp.full((8, width), -1e30, f32)
        l_ref[:, :width] = jnp.zeros((8, width), f32)
        c_ref[:, :width] = jnp.zeros((8, width), f32)
        dqt[:, :width] = jnp.zeros((HD, width), f32)

        def front(b, masked):
            at = pl.ds(pl.multiple_of(b * rows, rows), rows)
            s = dot_nt(k2[at, :], qs[:width, :])
            if masked:
                row_id = lax.rem(lax.broadcasted_iota(jnp.int32, (1, width), 1), rows)
                key_id = lax.broadcasted_iota(jnp.int32, (rows, width), 0)
                s = jnp.where(key_id <= row_id, s, -jnp.inf)
            d = dot_nt(vv[at, :], do_part[...])
            for n, (j, w) in enumerate(lanes):
                s_ref[b * len(lanes) + n, :, :w] = s[:, j:j + w]
                d_ref[b * len(lanes) + n, :, :w] = d[:, j:j + w]
            for n, (j, w) in enumerate(lanes):
                s = s_ref[b * len(lanes) + n, :, :w].reshape(rows // 8, 8, w)
                d = d_ref[b * len(lanes) + n, :, :w].reshape(rows // 8, 8, w)
                some = slice(j, j + w)
                old = m_ref[:, some]
                new = jnp.maximum(old, s.max(0))
                fade = jnp.exp2(old - new)
                e = jnp.exp2(s - new)
                l_ref[:, some] = l_ref[:, some] * fade + e.sum(0)
                c_ref[:, some] = c_ref[:, some] * fade + (e * d).sum(0)
                m_ref[:, some] = new

        in_groups(place, lambda b: front(b, False), sizes_of(width))
        front(place, True)
        top8 = m_ref[:, :width]
        top = top8.max(0, keepdims=True)
        fade = jnp.exp2(top8 - top)
        total = (l_ref[:, :width] * fade).sum(0, keepdims=True)
        m_ref[:, :width] = jnp.broadcast_to(top + jnp.log2(total), (8, width))
        l_ref[:, :width] = jnp.broadcast_to(
            (c_ref[:, :width] * fade).sum(0, keepdims=True) / total, (8, width))

    def finish(width, place, q_part, do_part, own_part):
        lanes = lanes_of(width)

        def back(b):
            at = pl.ds(pl.multiple_of(b * rows, rows), rows)
            ps, dss = [], []
            for n, (j, w) in enumerate(lanes):
                s = s_ref[b * len(lanes) + n, :, :w].reshape(rows // 8, 8, w)
                d = d_ref[b * len(lanes) + n, :, :w].reshape(rows // 8, 8, w)
                p = jnp.exp2(s - m_ref[:, j:j + w])
                ds = p * (d - l_ref[:, j:j + w])
                ps.append(p.reshape(rows, w).astype(bf16))
                dss.append(ds.reshape(rows, w).astype(bf16))
            p, ds = jnp.concatenate(ps, axis=1), jnp.concatenate(dss, axis=1)
            dv = jnp.dot(p, do_part[...], preferred_element_type=f32).reshape(Y, C, share, HD)
            dk = jnp.dot(ds, q_part[...], preferred_element_type=f32).reshape(Y, C, share, HD)
            if own_part:
                dv_acc[b] = dv
                dk_acc[b] = dk
            else:
                dv_acc[b] += dv
                dk_acc[b] += dk
            dqt[:, :width] += dot_tn(k2[at, :HD], ds)

        in_groups(place + 1, back, sizes_of(width))

    def head(h, carry):
        gather_c(h).wait_recv()

        @pl.loop(0, Z * X)
        def _(i):
            at = pl.ds(pl.multiple_of(i * rows, rows), rows)
            pair = kv[h, i // X, i % X].astype(f32)
            key = pair[:, :, :share].reshape(rows, HD).astype(bf16)
            k2[at, :HD] = key
            k2[at, HD:] = key
            vv[at, :] = pair[:, :, share:].reshape(rows, HD).astype(bf16)

        @pl.when(h >= 3)
        def _():
            sum_last(h - 3)

        def own(count):
            width = (groups - count) * rows
            return width, ctx, qf.at[h, :width], dof.at[h, :width]

        def foreign(count):
            width = count * rows
            return width, CTX - 1 - ctx, fq.at[h, :width], fdo.at[h, :width]

        def own_end(count):
            width = (groups - count) * rows
            finish(*own(count), True)

            @pl.when(h >= 2)
            def _():
                for g in range(groups - count):
                    write_dq(h - 2, g).wait()

            dq_st[h % 2, :width] = (dqt[:, :width] * scale).T.astype(bf16)
            for g in range(groups - count):
                write_dq(h, g).start()

            @pl.loop(ctx + 1, Z * X)
            def _(b):
                dv_acc[b] = jnp.zeros((Y, C, share, HD), f32)
                dk_acc[b] = jnp.zeros((Y, C, share, HD), f32)

        def foreign_begin(count):
            for i in range(count):
                shipped(h, i, count, 0).wait_recv()
                shipped(h, i, count, 1).wait_recv()
            begin(*foreign(count))

        def foreign_end(count):
            width = count * rows
            finish(*foreign(count), False)

            @pl.when(h >= 2)
            def _():
                for i in range(count):
                    returned(h - 2, i, count).wait_send()

            fdq_st[h % 2, :width] = (dqt[:, :width] * scale).T.astype(bf16)
            for i in range(count):
                returned(h, i, count).start()

        for is_owner, count in owners:
            @pl.when(is_owner)
            def _():
                for g in range(groups - count):
                    load(h, g, 0).wait()
                    load(h, g, 1).wait()
                begin(*own(count))

        @pl.when(ctx <= 1)
        def _():
            own_end(0)
            foreign_begin(2)

        for following in range(1, heads):
            @pl.when(h == following - 1)
            def _():
                end(following, 1)
                gather_c(following).start()
                if following == 1:
                    end(3, 0)
                    start(3, 1)

        @pl.when(h >= 1)
        def _():
            sum_second(h - 1)

        @pl.when(h >= 2)
        def _():
            sum_third(h - 2)

        for is_owner, count in owners:
            @pl.when(jnp.logical_and(is_owner, ctx >= 2))
            def _():
                own_end(count)

        @pl.when(ctx <= 1)
        def _():
            foreign_end(2)

        @pl.when(ctx == 2)
        def _():
            foreign_begin(1)
            foreign_end(1)

        sum_first(h)
        return carry

    lax.fori_loop(0, heads, head, 0)

    tail_first()
    sum_last(last - 2)
    sum_third(last - 1)
    sum_last(last - 1)
    tail_second()
    tail_third()
    for d in range(1, Y):
        tail_y(d).wait_send()
        tail_y_first(d).wait_send()
    for i in range(len(others)):
        tail_b(i).wait_send()
        tail_b_last(i).wait_send()
    for h in range(heads):
        gather_c(h).wait_send()
        for move in moves(h, 0) + moves(h, 1):
            move.wait_send()
    sum_c(last).wait_send()
    for is_owner, count in owners:
        @pl.when(is_owner)
        def _():
            for h in range(heads):
                for i in range(count):
                    shipped(h, i, count, 0).wait_send()
                    shipped(h, i, count, 1).wait_send()
                    returned(h, i, count).wait_recv()
            for h in (last - 1, last):
                for g in range(groups - count):
                    write_dq(h, g).wait()
    for is_helper, count in helpers:
        @pl.when(is_helper)
        def _():
            for h in (last - 1, last):
                for i in range(count):
                    returned(h, i, count).wait_send()


def shards(queries, out_grad, keys, values):
    _, rows, cols = queries.shape
    share, key_cols = keys.shape
    heads = key_cols // HD
    groups = cols // key_cols
    flat = rows * groups
    seq = rows * Z * X
    pair = (2 * share, HD)
    V = pltpu.VMEM
    sem = pltpu.SemaphoreType.DMA
    any_space = pl.BlockSpec(memory_space=pl.ANY)
    in_vmem = pl.BlockSpec(memory_space=pltpu.VMEM)
    dq, dk, dv = pl.pallas_call(
        kernel,
        in_specs=[any_space, any_space, in_vmem, in_vmem],
        out_specs=[any_space, in_vmem, in_vmem],
        out_shape=[jax.ShapeDtypeStruct((rows, cols), bf16),
                   jax.ShapeDtypeStruct((share, key_cols), bf16),
                   jax.ShapeDtypeStruct((share, key_cols), bf16)],
        scratch_shapes=[
            V((heads, Z, X, Y, C) + pair, bf16),
            V((heads, flat, HD), bf16), V((heads, flat, HD), bf16),
            V((heads, 2 * rows, HD), bf16), V((heads, 2 * rows, HD), bf16),
            V((flat, 2 * HD), bf16), V((seq, 2 * HD), bf16), V((seq, HD), bf16),
            V((65, rows, HD), f32), V((65, rows, HD), f32),
            V((8, flat), f32), V((8, flat), f32), V((8, flat), f32),
            V((HD, flat), f32), V((2, flat, HD), bf16), V((2, 2 * rows, HD), bf16),
            V((Z * X, Y, C, share, HD), f32), V((Z * X, Y, C, share, HD), f32),
            V((Z, X, Y) + pair, f32), V((2, Y) + pair, f32), V((Y,) + pair, f32),
            V((Z, X, Y) + pair, bf16), V((2, Z, X, Y) + pair, bf16),
            V((Z * X - 1, Y) + pair, bf16), V((heads, Z * X - 1, Y) + pair, bf16),
            V((Y - 1,) + pair, bf16), V((heads, Y - 1) + pair, bf16),
            V((Z, X, 2 * share - CUT, HD), f32),
            V((Y - 1, Z, X, 2 * share - CUT, HD), bf16), V((Y - 1, Z, X, 2 * share - CUT, HD), bf16),
            V((Z * X - 1, 2 * share - CUT, HD), bf16), V((Z * X - 1, 2 * share - CUT, HD), bf16),
            sem((2, heads, groups)), sem((2, groups)), sem((2, 2, heads, 2)), sem((2, heads, 2)),
            sem((2, heads, Y - 1)), sem((2, heads, Z * X - 1)), sem((2, heads)),
            sem((2, heads)), sem((2, heads, Z * X - 1)), sem((2, heads, Y - 1)),
            sem((2, Y - 1)), sem((2, Z * X - 1)),
        ],
        compiler_params=pltpu.CompilerParams(
            collective_id=0, has_side_effects=True, vmem_limit_bytes=65400 << 10),
    )(queries[0], out_grad[0], keys, values)
    return dq[None], dk, dv


def solution(mesh):
    wide = P("section", "ctx", "head")
    tall = P(("section", "ctx"), "head")
    return jax.shard_map(shards, mesh=mesh, in_specs=(wide, wide, tall, tall),
                         out_specs=(wide, tall, tall), check_vma=False)
```

```python
import functools

import jax
import jax.numpy as jnp
from jax import lax
from jax.experimental import pallas as pl
from jax.experimental.pallas import tpu as pltpu
from jax.sharding import PartitionSpec as P

HD = 128
LOG2E = 1.4426950408889634
bf16, f32 = jnp.bfloat16, jnp.float32
MESH = pl.DeviceIdType.MESH
Z, X, Y, C = 4, 2, 4, 2


def dot_nt(a, b):
    return lax.dot_general(a, b, (((1,), (1,)), ((), ())), preferred_element_type=f32)


def dot_tn(a, b):
    return lax.dot_general(a, b, (((0,), (0,)), ((), ())), preferred_element_type=f32)


def in_groups(count, step, sizes):
    done = 0
    for size in sizes:
        @pl.loop(done // size, count // size)
        def _(i):
            for n in range(size):
                step(size * i + n)

        done = count // size * size


CTX = Y * C
ALONG_Y_LAST = (1, 3)
CUT = 48
SHIP = ((0, 4, 0), (5, 5, 1), (6, 7, 2))


def kernel(q_hbm, do_hbm, k_in, v_in, dq_hbm, dk_out, dv_out,
           kv, qf, dof, fq, fdo, qs, k2, vv, s_ref, d_ref, m_ref, l_ref, c_ref, dqt, dq_st, fdq_st,
           dk_acc, dv_acc, own_sum, keep_b, keep_y, cs, cr, bs, br, ys, yr, keep_t, ty, tyr, tb, tbr,
           in_sem, dq_sem, ship_sem, back_sem, gy, gb, gc, rc, rb, ry, ra, rc2):
    rows = q_hbm.shape[0]
    share = k_in.shape[0]
    heads = k_in.shape[1] // HD
    groups = q_hbm.shape[1] // k_in.shape[1]
    flat = rows * groups
    last = heads - 1
    scale = HD ** -0.5
    section, ctx, half = lax.axis_index("section"), lax.axis_index("ctx"), lax.axis_index("head")
    z, x, y, c = section // X, section % X, ctx // C, ctx % C

    def device(z, x, y, c):
        return (z * X + x, y * C + c, half)

    y_at = [device(z, x, (y + d) % Y, c) for d in range(1, Y)]
    c_at = device(z, x, y, 1 - c)
    others = [(dz, dx) for dz in range(Z) for dx in range(X) if dz or dx]
    block_of = [((z + dz) % Z, (x + dx) % X) for dz, dx in others]
    block_at = [device(bz, bx, y, c) for bz, bx in block_of]

    def load(h, g, which):
        source, target = ((q_hbm, qf), (do_hbm, dof))[which]
        cols = pl.ds(pl.multiple_of((h * groups + g) * HD, HD), HD)
        return pltpu.make_async_copy(
            source.at[:, cols], target.at[h, pl.ds(g * rows, rows), :], in_sem.at[which, h, g])

    mirror = (section, CTX - 1 - ctx, half)

    def shipped(h, i, count, which):
        source, target = ((q_hbm, fq), (do_hbm, fdo))[which]
        cols = pl.ds(pl.multiple_of(((h + 1) * groups - count + i) * HD, HD), HD)
        return pltpu.make_async_remote_copy(
            src_ref=source.at[:, cols], dst_ref=target.at[h, pl.ds(i * rows, rows), :],
            send_sem=ship_sem.at[0, which, h, i], recv_sem=ship_sem.at[1, which, h, i],
            device_id=mirror, device_id_type=MESH)

    def returned(h, i, count):
        cols = pl.ds(pl.multiple_of(((h + 1) * groups - count + i) * HD, HD), HD)
        return pltpu.make_async_remote_copy(
            src_ref=fdq_st.at[h % 2, pl.ds(i * rows, rows), :], dst_ref=dq_hbm.at[:, cols],
            send_sem=back_sem.at[0, h, i], recv_sem=back_sem.at[1, h, i],
            device_id=mirror, device_id_type=MESH)

    owners = [(low <= ctx, ctx <= high, count) for low, high, count in SHIP]
    owners = [(jnp.logical_and(over, under), count) for over, under, count in owners]
    helpers = [(low <= CTX - 1 - ctx, CTX - 1 - ctx <= high, count) for low, high, count in SHIP]
    helpers = [(jnp.logical_and(over, under), count) for over, under, count in helpers if count]

    barrier = pltpu.get_barrier_semaphore()
    partners = y_at + block_at + [c_at, mirror]
    for partner in partners:
        pl.semaphore_signal(barrier, inc=1, device_id=partner, device_id_type=MESH)
    for is_owner, count in owners:
        @pl.when(is_owner)
        def _():
            for g in range(groups - count):
                load(0, g, 0).start()
                load(0, g, 1).start()

    for h in range(heads):
        cols = slice(h * HD, (h + 1) * HD)
        pair = jnp.concatenate([k_in[:, cols].astype(f32), v_in[:, cols].astype(f32)], axis=0)
        kv[h, z, x, y, c] = pair.astype(bf16)
    pl.semaphore_wait(barrier, len(partners))

    def copy(src, dst, sems, index, where):
        return pltpu.make_async_remote_copy(
            src_ref=src, dst_ref=dst, send_sem=sems.at[(0,) + index], recv_sem=sems.at[(1,) + index],
            device_id=where, device_id_type=MESH)

    def gather_y(h, d):
        part = kv.at[h, :, :, y, c] if h in ALONG_Y_LAST else kv.at[h, z, x, y, c]
        return copy(part, part, gy, (h, d - 1), y_at[d - 1])

    def gather_b(h, i):
        part = kv.at[h, z, x, y, c] if h in ALONG_Y_LAST else kv.at[h, z, x, :, c]
        return copy(part, part, gb, (h, i), block_at[i])

    def gather_c(h):
        part = kv.at[h, :, :, :, c]
        return copy(part, part, gc, (h,), c_at)

    def moves(h, step):
        if (h in ALONG_Y_LAST) == (step == 0):
            return [gather_b(h, i) for i in range(len(others))]
        return [gather_y(h, d) for d in range(1, Y)]

    def start(h, step):
        for move in moves(h, step):
            move.start()

    def end(h, step):
        for move in moves(h, step):
            move.wait_recv()

    def ship(heads_now):
        for is_owner, count in owners:
            if count:
                @pl.when(is_owner)
                def _():
                    for h in heads_now:
                        for i in range(count):
                            shipped(h, i, count, 0).start()
                            shipped(h, i, count, 1).start()

    start(0, 0)
    start(1, 0)
    ship([0])
    end(0, 0)
    start(0, 1)
    for is_owner, count in owners:
        @pl.when(is_owner)
        def _():
            for h in range(1, heads):
                for g in range(groups - count):
                    load(h, g, 0).start()
                    load(h, g, 1).start()

    end(1, 0)
    start(1, 1)
    start(2, 0)
    start(3, 0)
    ship([1])
    end(0, 1)
    gather_c(0).start()
    end(2, 0)
    start(2, 1)
    ship(range(2, heads))

    def sum_c(h):
        return copy(cs, cr.at[h % 2], rc, (h,), c_at)

    def sum_b(h, i):
        return copy(bs.at[i], br.at[h, i], rb, (h, i), block_at[i])

    def sum_y(h, d):
        return copy(ys.at[d - 1], yr.at[h, d - 1], ry, (h, d - 1), y_at[d - 1])

    def sum_first(h):
        @pl.when(h >= 1)
        def _():
            sum_c(h - 1).wait_send()

        for i in range(Z * X):
            for core, put in ((1 - c, True), (c, False)):
                pair = jnp.concatenate([dk_acc[i, :, core], dv_acc[i, :, core]], axis=1)
                if put:
                    cs[i // X, i % X] = pair.astype(bf16)
                else:
                    own_sum[i // X, i % X] = pair
        sum_c(h).start()

    def sum_second(h):
        sum_c(h).wait_recv()

        @pl.when(h >= 1)
        def _():
            for i in range(len(others)):
                sum_b(h - 1, i).wait_send()

        for i, (bz, bx) in enumerate(block_of):
            bs[i] = (own_sum[bz, bx] + cr[h % 2, bz, bx].astype(f32)).astype(bf16)
            sum_b(h, i).start()
        keep_b[h % 2] = own_sum[z, x] + cr[h % 2, z, x].astype(f32)

    def sum_third(h):
        total = keep_b[h % 2]
        for i in range(len(others)):
            sum_b(h, i).wait_recv()
            total = total + br[h, i].astype(f32)

        @pl.when(h >= 1)
        def _():
            for d in range(1, Y):
                sum_y(h - 1, d).wait_send()

        keep_y[...] = total
        for d in range(1, Y):
            ys[d - 1] = keep_y[(y + d) % Y].astype(bf16)
            sum_y(h, d).start()

    def sum_last(h):
        total = keep_y[y]
        for d in range(1, Y):
            sum_y(h, d).wait_recv()
            total = total + yr[h, d - 1].astype(f32)
        write_out(h, total)

    def write_out(h, total):
        cols = pl.ds(pl.multiple_of(h * HD, HD), HD)
        dk_out[:, cols] = (total[:share] * scale).astype(bf16)
        dv_out[:, cols] = total[share:].astype(bf16)

    def head_rows(ref):
        return ref.at[:, pl.ds(0, CUT), :]

    def tail_b(i):
        return copy(head_rows(bs.at[i]), head_rows(br.at[last, i]), rb, (last, i), block_at[i])

    def tail_y(d):
        return copy(ys.at[d - 1, pl.ds(0, CUT), :], yr.at[last, d - 1, pl.ds(0, CUT), :], ry,
                    (last, d - 1), y_at[d - 1])

    def tail_y_first(d):
        return copy(ty.at[d - 1], tyr.at[d - 1], ra, (d - 1,), y_at[d - 1])

    def tail_b_last(i):
        return copy(tb.at[i], tbr.at[i], rc2, (i,), block_at[i])

    def tail_first():
        for i in range(len(others)):
            sum_b(last - 1, i).wait_send()
        sum_c(last).wait_recv()
        slot = last % 2
        for d in range(1, Y):
            at = (y + d) % Y
            ty[d - 1] = (own_sum[:, :, at, CUT:] + cr[slot, :, :, at, CUT:].astype(f32)).astype(bf16)
            tail_y_first(d).start()
        for i, (bz, bx) in enumerate(block_of):
            bs[i, :, :CUT] = (own_sum[bz, bx, :, :CUT] + cr[slot, bz, bx, :, :CUT].astype(f32)).astype(bf16)
            tail_b(i).start()
        keep_b[slot, :, :CUT] = own_sum[z, x, :, :CUT] + cr[slot, z, x, :, :CUT].astype(f32)
        keep_t[...] = own_sum[:, :, y, CUT:] + cr[slot, :, :, y, CUT:].astype(f32)

    def tail_second():
        total = keep_t[...]
        for d in range(1, Y):
            tail_y_first(d).wait_recv()
            total = total + tyr[d - 1].astype(f32)
        keep_t[...] = total
        for i, (bz, bx) in enumerate(block_of):
            tb[i] = keep_t[bz, bx].astype(bf16)
            tail_b_last(i).start()
        total = keep_b[last % 2, :, :CUT]
        for i in range(len(others)):
            tail_b(i).wait_recv()
            total = total + br[last, i, :, :CUT].astype(f32)
        keep_y[:, :CUT] = total
        for d in range(1, Y):
            sum_y(last - 1, d).wait_send()
            ys[d - 1, :CUT] = keep_y[(y + d) % Y, :CUT].astype(bf16)
            tail_y(d).start()

    def tail_third():
        below = keep_t[z, x]
        for i in range(len(others)):
            tail_b_last(i).wait_recv()
            below = below + tbr[i].astype(f32)
        above = keep_y[y, :CUT]
        for d in range(1, Y):
            tail_y(d).wait_recv()
            above = above + yr[last, d - 1, :CUT].astype(f32)
        write_out(last, jnp.concatenate([above, below], axis=0))

    def write_dq(h, g):
        cols = pl.ds(pl.multiple_of((h * groups + g) * HD, HD), HD)
        return pltpu.make_async_copy(
            dq_st.at[h % 2, pl.ds(g * rows, rows), :], dq_hbm.at[:, cols], dq_sem.at[h % 2, g])

    def lanes_of(width):
        return [(j, min(HD, width - j)) for j in range(0, width, HD)]

    def sizes_of(width):
        return (4, 2, 1) if width <= 3 * rows else (2, 1)

    def begin(width, place, q_part, do_part):
        lanes = lanes_of(width)
        wide = q_part[...].astype(f32) * (scale * LOG2E)
        high = wide.astype(bf16)
        qs[:width, :HD] = high
        qs[:width, HD:] = (wide - high.astype(f32)).astype(bf16)
        m_ref[:, :width] = jnp.full((8, width), -1e30, f32)
        l_ref[:, :width] = jnp.zeros((8, width), f32)
        c_ref[:, :width] = jnp.zeros((8, width), f32)
        dqt[:, :width] = jnp.zeros((HD, width), f32)

        def front(b, masked):
            at = pl.ds(pl.multiple_of(b * rows, rows), rows)
            s = dot_nt(k2[at, :], qs[:width, :])
            if masked:
                row_id = lax.rem(lax.broadcasted_iota(jnp.int32, (1, width), 1), rows)
                key_id = lax.broadcasted_iota(jnp.int32, (rows, width), 0)
                s = jnp.where(key_id <= row_id, s, -jnp.inf)
            d = dot_nt(vv[at, :], do_part[...])
            for n, (j, w) in enumerate(lanes):
                s_ref[b * len(lanes) + n, :, :w] = s[:, j:j + w]
                d_ref[b * len(lanes) + n, :, :w] = d[:, j:j + w]
            for n, (j, w) in enumerate(lanes):
                s = s_ref[b * len(lanes) + n, :, :w].reshape(rows // 8, 8, w)
                d = d_ref[b * len(lanes) + n, :, :w].reshape(rows // 8, 8, w)
                some = slice(j, j + w)
                old = m_ref[:, some]
                new = jnp.maximum(old, s.max(0))
                fade = jnp.exp2(old - new)
                e = jnp.exp2(s - new)
                l_ref[:, some] = l_ref[:, some] * fade + e.sum(0)
                c_ref[:, some] = c_ref[:, some] * fade + (e * d).sum(0)
                m_ref[:, some] = new

        in_groups(place, lambda b: front(b, False), sizes_of(width))
        front(place, True)
        top8 = m_ref[:, :width]
        top = top8.max(0, keepdims=True)
        fade = jnp.exp2(top8 - top)
        total = (l_ref[:, :width] * fade).sum(0, keepdims=True)
        m_ref[:, :width] = jnp.broadcast_to(top + jnp.log2(total), (8, width))
        l_ref[:, :width] = jnp.broadcast_to(
            (c_ref[:, :width] * fade).sum(0, keepdims=True) / total, (8, width))

    def finish(width, place, q_part, do_part, own_part):
        lanes = lanes_of(width)

        def back(b):
            at = pl.ds(pl.multiple_of(b * rows, rows), rows)
            ps, dss = [], []
            for n, (j, w) in enumerate(lanes):
                s = s_ref[b * len(lanes) + n, :, :w].reshape(rows // 8, 8, w)
                d = d_ref[b * len(lanes) + n, :, :w].reshape(rows // 8, 8, w)
                p = jnp.exp2(s - m_ref[:, j:j + w])
                ds = p * (d - l_ref[:, j:j + w])
                ps.append(p.reshape(rows, w).astype(bf16))
                dss.append(ds.reshape(rows, w).astype(bf16))
            p, ds = jnp.concatenate(ps, axis=1), jnp.concatenate(dss, axis=1)
            dv = jnp.dot(p, do_part[...], preferred_element_type=f32).reshape(Y, C, share, HD)
            dk = jnp.dot(ds, q_part[...], preferred_element_type=f32).reshape(Y, C, share, HD)
            if own_part:
                dv_acc[b] = dv
                dk_acc[b] = dk
            else:
                dv_acc[b] += dv
                dk_acc[b] += dk
            dqt[:, :width] += dot_tn(k2[at, :HD], ds)

        in_groups(place + 1, back, sizes_of(width))

    def head(h, carry):
        gather_c(h).wait_recv()

        @pl.loop(0, Z * X)
        def _(i):
            at = pl.ds(pl.multiple_of(i * rows, rows), rows)
            pair = kv[h, i // X, i % X].astype(f32)
            key = pair[:, :, :share].reshape(rows, HD).astype(bf16)
            k2[at, :HD] = key
            k2[at, HD:] = key
            vv[at, :] = pair[:, :, share:].reshape(rows, HD).astype(bf16)

        @pl.when(h >= 3)
        def _():
            sum_last(h - 3)

        def own(count):
            width = (groups - count) * rows
            return width, ctx, qf.at[h, :width], dof.at[h, :width]

        def foreign(count):
            width = count * rows
            return width, CTX - 1 - ctx, fq.at[h, :width], fdo.at[h, :width]

        def own_end(count):
            width = (groups - count) * rows
            finish(*own(count), True)

            @pl.when(h >= 2)
            def _():
                for g in range(groups - count):
                    write_dq(h - 2, g).wait()

            dq_st[h % 2, :width] = (dqt[:, :width] * (scale / 2)).T.astype(bf16)
            for g in range(groups - count):
                write_dq(h, g).start()

            @pl.loop(ctx + 1, Z * X)
            def _(b):
                dv_acc[b] = jnp.zeros((Y, C, share, HD), f32)
                dk_acc[b] = jnp.zeros((Y, C, share, HD), f32)

        def foreign_begin(count):
            for i in range(count):
                shipped(h, i, count, 0).wait_recv()
                shipped(h, i, count, 1).wait_recv()
            begin(*foreign(count))

        def foreign_end(count):
            width = count * rows
            finish(*foreign(count), False)

            @pl.when(h >= 2)
            def _():
                for i in range(count):
                    returned(h - 2, i, count).wait_send()

            fdq_st[h % 2, :width] = (dqt[:, :width] * (scale / 2)).T.astype(bf16)
            for i in range(count):
                returned(h, i, count).start()

        for is_owner, count in owners:
            @pl.when(is_owner)
            def _():
                for g in range(groups - count):
                    load(h, g, 0).wait()
                    load(h, g, 1).wait()
                begin(*own(count))

        @pl.when(ctx <= 1)
        def _():
            own_end(0)
            foreign_begin(2)

        for following in range(1, heads):
            @pl.when(h == following - 1)
            def _():
                end(following, 1)
                gather_c(following).start()
                if following == 1:
                    end(3, 0)
                    start(3, 1)

        @pl.when(h >= 1)
        def _():
            sum_second(h - 1)

        @pl.when(h >= 2)
        def _():
            sum_third(h - 2)

        for is_owner, count in owners:
            @pl.when(jnp.logical_and(is_owner, ctx >= 2))
            def _():
                own_end(count)

        @pl.when(ctx <= 1)
        def _():
            foreign_end(2)

        @pl.when(ctx == 2)
        def _():
            foreign_begin(1)
            foreign_end(1)

        sum_first(h)
        return carry

    lax.fori_loop(0, heads, head, 0)

    tail_first()
    sum_last(last - 2)
    sum_third(last - 1)
    sum_last(last - 1)
    tail_second()
    tail_third()
    for d in range(1, Y):
        tail_y(d).wait_send()
        tail_y_first(d).wait_send()
    for i in range(len(others)):
        tail_b(i).wait_send()
        tail_b_last(i).wait_send()
    for h in range(heads):
        gather_c(h).wait_send()
        for move in moves(h, 0) + moves(h, 1):
            move.wait_send()
    sum_c(last).wait_send()
    for is_owner, count in owners:
        @pl.when(is_owner)
        def _():
            for h in range(heads):
                for i in range(count):
                    shipped(h, i, count, 0).wait_send()
                    shipped(h, i, count, 1).wait_send()
                    returned(h, i, count).wait_recv()
            for h in (last - 1, last):
                for g in range(groups - count):
                    write_dq(h, g).wait()
    for is_helper, count in helpers:
        @pl.when(is_helper)
        def _():
            for h in (last - 1, last):
                for i in range(count):
                    returned(h, i, count).wait_send()


def shards(queries, out_grad, keys, values):
    _, rows, cols = queries.shape
    share, key_cols = keys.shape
    heads = key_cols // HD
    groups = cols // key_cols
    flat = rows * groups
    seq = rows * Z * X
    pair = (2 * share, HD)
    V = pltpu.VMEM
    sem = pltpu.SemaphoreType.DMA
    any_space = pl.BlockSpec(memory_space=pl.ANY)
    in_vmem = pl.BlockSpec(memory_space=pltpu.VMEM)
    dq, dk, dv = pl.pallas_call(
        kernel,
        in_specs=[any_space, any_space, in_vmem, in_vmem],
        out_specs=[any_space, in_vmem, in_vmem],
        out_shape=[jax.ShapeDtypeStruct((rows, cols), bf16),
                   jax.ShapeDtypeStruct((share, key_cols), bf16),
                   jax.ShapeDtypeStruct((share, key_cols), bf16)],
        scratch_shapes=[
            V((heads, Z, X, Y, C) + pair, bf16),
            V((heads, flat, HD), bf16), V((heads, flat, HD), bf16),
            V((heads, 2 * rows, HD), bf16), V((heads, 2 * rows, HD), bf16),
            V((flat, 2 * HD), bf16), V((seq, 2 * HD), bf16), V((seq, HD), bf16),
            V((65, rows, HD), f32), V((65, rows, HD), f32),
            V((8, flat), f32), V((8, flat), f32), V((8, flat), f32),
            V((HD, flat), f32), V((2, flat, HD), bf16), V((2, 2 * rows, HD), bf16),
            V((Z * X, Y, C, share, HD), f32), V((Z * X, Y, C, share, HD), f32),
            V((Z, X, Y) + pair, f32), V((2, Y) + pair, f32), V((Y,) + pair, f32),
            V((Z, X, Y) + pair, bf16), V((2, Z, X, Y) + pair, bf16),
            V((Z * X - 1, Y) + pair, bf16), V((heads, Z * X - 1, Y) + pair, bf16),
            V((Y - 1,) + pair, bf16), V((heads, Y - 1) + pair, bf16),
            V((Z, X, 2 * share - CUT, HD), f32),
            V((Y - 1, Z, X, 2 * share - CUT, HD), bf16), V((Y - 1, Z, X, 2 * share - CUT, HD), bf16),
            V((Z * X - 1, 2 * share - CUT, HD), bf16), V((Z * X - 1, 2 * share - CUT, HD), bf16),
            sem((2, heads, groups)), sem((2, groups)), sem((2, 2, heads, 2)), sem((2, heads, 2)),
            sem((2, heads, Y - 1)), sem((2, heads, Z * X - 1)), sem((2, heads)),
            sem((2, heads)), sem((2, heads, Z * X - 1)), sem((2, heads, Y - 1)),
            sem((2, Y - 1)), sem((2, Z * X - 1)),
        ],
        compiler_params=pltpu.CompilerParams(
            collective_id=0, has_side_effects=True, vmem_limit_bytes=65400 << 10),
    )(queries[0], out_grad[0], keys, values)
    return (dq * 2)[None], dk, dv


def solution(mesh):
    wide = P("section", "ctx", "head")
    tall = P(("section", "ctx"), "head")
    return jax.shard_map(shards, mesh=mesh, in_specs=(wide, wide, tall, tall),
                         out_specs=(wide, tall, tall), check_vma=False)
```
